256 devices in a mesh: row: 32 (over y, z_lo, core), col: 8 (over x, z_hi).
Axes of the slice: x: 4, y: 4, z: 8 (z_hi: 2, z_lo: 4; z = z_hi * 4 + z_lo), core: 2. Of those that a mesh axis runs over, the one named last changes fastest.
Arguments:
- features: bfloat16 [131072, 128], P(('col', 'row')), may hold values from -6 to 6
- weight: bfloat16 [128, 172], replicated, may hold values from -0.5 to 0.5
- labels: int32 [131072], P(('row', 'col')), may hold values from -43 to 171
- tile_rows: int32 [32, 8, 256], P('row', 'col'), may hold values from 0 to 31, as said below
- tile_cols: int32 [32, 8, 256], P('row', 'col'), may hold values from 0 to 127
- tile_count: int32 [32, 8], P('row', 'col'), may hold values from 1 to 256, as said below
- tile_vals: bfloat16 [32, 8, 256, 128, 128], P('row', 'col'), may hold values from -0.07470703 to 0.07470703
Outputs:
- logits: float32 [131072, 172], P(('row', 'col'))
- weight_grad: float32 [128, 172], replicated
The draws below stay inside these ranges and needn't reach their ends.
Inputs may be any that keep to these rules, and one draw needn't show every extreme that they name: `tile_rows`: within one device the used slots name distinct tiles; unused slots are ignored. `tile_count`: counts differ between devices; in every draw some device uses all 256 slots.
All inputs are finite; a program needn't handle non-finite values.
Results may differ from the reference program's by a relative error of at most 0.0029.
Values may be sent and summed in bfloat16 or wider, within the bound.
No kernel may reach another device: no remote copies, remote signals or barrier semaphores. Data moves between devices by JAX's collectives and lax.ppermute only.
A program may use at most 128 MiB of HBM per device.

```python
import jax
import jax.numpy as jnp
from jax import lax

FEAT = 128
CLASSES = 172
TILE = 128
TMAX = 256
ROW_TILES = 32
COL_TILES = 128
NODES = 131072
N_ROW = 32
N_COL = 8


def tile_places(key):
    keys = jax.random.split(key, N_ROW * N_COL)
    picked = jax.vmap(lambda k: jax.random.permutation(k, ROW_TILES * COL_TILES)[:TMAX])(keys)
    return picked.reshape(N_ROW, N_COL, TMAX).astype(jnp.int32)


def draw_tile_rows(key, part):
    return tile_places(key) // COL_TILES


def draw_tile_cols(key, part):
    return tile_places(key) % COL_TILES


def draw_tile_count(key, part):
    key = jax.random.fold_in(key, 7)
    key_a, key_b = jax.random.split(key)
    counts = jax.random.randint(key_a, (N_ROW * N_COL,), max(1, TMAX // 8), TMAX // 2 + 1)
    busiest = jax.random.randint(key_b, (), 0, N_ROW * N_COL)
    counts = jnp.where(jnp.arange(N_ROW * N_COL) == busiest, TMAX, counts)
    return counts.reshape(N_ROW, N_COL).astype(jnp.int32)


def plant(entries, rng, smallest, top_value):
    dims = entries.shape
    spot = [jax.random.randint(jax.random.fold_in(rng, axis), (), 0, dims[axis]) for axis in range(len(dims))]
    entries = entries.at[tuple(spot)].set(smallest)
    longest = dims.index(max(dims))
    spot[longest] = (spot[longest] + 1) % dims[longest]
    return entries.at[tuple(spot)].set(top_value)


def block_scale(rng, dims, pieces, low, largest):
    level, own = 1.0, jax.random.fold_in(rng, 6)
    for dim, blocks in pieces:
        steps = jnp.exp(jax.random.uniform(jax.random.fold_in(own, dim), (blocks,), jnp.float32, low / len(pieces), largest / len(pieces)))
        level = level * jnp.repeat(steps, dims[dim] // blocks).reshape([-1 if axis == dim else 1 for axis in range(len(dims))])
    return level


def gaussian(rng, shape, spread, most, cuts=(), held_as=jnp.bfloat16):
    entries = spread * jax.random.normal(rng, shape, jnp.float32)
    if cuts:
        entries = entries * block_scale(rng, shape, cuts, -0.22, 0.18)
    return jnp.clip(entries, -most, most).astype(held_as)


def setup_inputs(seed: int = 0) -> dict:
    streams_of = jax.random.split(jax.random.key(seed), 8)
    features = gaussian(streams_of[0], (NODES, FEAT), 1.0, 6.0, ((0, 256),))
    weight = gaussian(streams_of[1], (FEAT, CLASSES), FEAT ** -0.5, 0.5)
    labels = plant(jax.random.randint(streams_of[2], (NODES,), 0 - CLASSES // 4, CLASSES), jax.random.fold_in(streams_of[2], 1), 0 - CLASSES // 4, CLASSES - 1).astype(jnp.int32)
    tile_rows = draw_tile_rows(jax.random.fold_in(streams_of[7], 71), 0)
    tile_cols = draw_tile_cols(jax.random.fold_in(streams_of[7], 71), 0)
    tile_count = draw_tile_count(jax.random.fold_in(streams_of[7], 71), 0)
    tile_vals = gaussian(streams_of[6], (N_ROW, N_COL, TMAX, TILE, TILE), 0.0125, 0.07470703, ((0, 32), (1, 8)))
    return {"features": features, "weight": weight, "labels": labels, "tile_rows": tile_rows, "tile_cols": tile_cols, "tile_count": tile_count, "tile_vals": tile_vals}


def aggregate(table, gather_idx, scatter_idx, vals, count, out_tiles, transpose):
    blk = min(32, vals.shape[0])
    classes = table.shape[-1]
    nblk = (count + blk - 1) // blk

    def step(b, acc):
        start = (b * blk).astype(jnp.int32)
        piece = lax.dynamic_slice_in_dim(vals, start, blk, 0).astype(jnp.float32)
        gidx = lax.dynamic_slice_in_dim(gather_idx, start, blk, 0)
        sidx = lax.dynamic_slice_in_dim(scatter_idx, start, blk, 0)
        sel = table[gidx].astype(jnp.float32)
        if transpose:
            prod = jnp.einsum('tji,tjc->tic', piece, sel)
        else:
            prod = jnp.einsum('tij,tjc->tic', piece, sel)
        valid = (start + jnp.arange(blk, dtype=jnp.int32) < count).astype(jnp.float32)
        return acc.at[sidx].add(prod * valid[:, None, None])
    init = jnp.zeros((out_tiles, table.shape[1], classes), jnp.float32)
    return lax.fori_loop(0, nblk, step, init)

def reference(features, weight, labels, tile_rows, tile_cols, tile_count, tile_vals):
    classes = weight.shape[1]
    row_len = ROW_TILES * TILE
    col_len = COL_TILES * TILE
    projected = jnp.dot(features, weight, preferred_element_type=jnp.float32).astype(jnp.bfloat16)

    def forward(idx, acc):
        r = idx // N_COL
        c = idx % N_COL
        block = lax.dynamic_slice_in_dim(projected, (c * col_len).astype(jnp.int32), col_len, 0)
        table = block.reshape(COL_TILES, TILE, classes)
        part = aggregate(table, tile_cols[r, c], tile_rows[r, c], tile_vals[r, c], tile_count[r, c], ROW_TILES, False)
        start = (r * row_len).astype(jnp.int32)
        old = lax.dynamic_slice_in_dim(acc, start, row_len, 0)
        return lax.dynamic_update_slice_in_dim(acc, old + part.reshape(row_len, classes), start, 0)
    logits = lax.fori_loop(0, N_ROW * N_COL, forward, jnp.zeros((NODES, classes), jnp.float32))
    onehot = (labels[:, None] == jnp.arange(classes, dtype=jnp.int32)[None, :]).astype(jnp.float32)
    residual_grad = jnp.where(labels[:, None] >= 0, logits - onehot, 0.0).astype(jnp.bfloat16)

    def backward(idx, acc):
        r = idx // N_COL
        c = idx % N_COL
        block = lax.dynamic_slice_in_dim(residual_grad, (r * row_len).astype(jnp.int32), row_len, 0)
        table = block.reshape(ROW_TILES, TILE, classes)
        part = aggregate(table, tile_rows[r, c], tile_cols[r, c], tile_vals[r, c], tile_count[r, c], COL_TILES, True)
        start = (c * col_len).astype(jnp.int32)
        old = lax.dynamic_slice_in_dim(acc, start, col_len, 0)
        return lax.dynamic_update_slice_in_dim(acc, old + part.reshape(col_len, classes), start, 0)
    projected_grad = lax.fori_loop(0, N_ROW * N_COL, backward, jnp.zeros((NODES, classes), jnp.float32))
    weight_grad = jnp.dot(features.astype(jnp.float32).T, projected_grad, precision=lax.Precision.HIGHEST)
    weight_grad = weight_grad / jnp.sqrt(jnp.float32(NODES))
    return (logits, weight_grad)
```

```python
import math

import jax
import jax.numpy as jnp
from jax import lax
from jax.experimental import pallas as pl
from jax.experimental.pallas import tpu as pltpu
from jax.sharding import Mesh, PartitionSpec as P

AXES = ("y", "zl", "core", "x", "zh")
SIZES = (4, 4, 2, 4, 2)
ROW = AXES[:3]
COL = AXES[3:]
GROUP = 8
CHUNK = 32


def shift(value, axes, step):
    n = lax.axis_size(axes)
    return lax.ppermute(value, axes, [(i, (i + step) % n) for i in range(n)])


def aggregate_kernel(count_ref, rows_ref, places_ref, mine_ref, other_ref, vals_ref, out_ref,
                     table, vals, acc, prods, sem_table, sem_vals):
    tile = vals.shape[-1]
    half = mine_ref.shape[0]
    chunks = vals.shape[0] // CHUNK
    count = count_ref[0]

    def vals_copy(k):
        part = pl.ds(k * CHUNK, CHUNK)
        return pltpu.make_async_copy(vals_ref.at[part], vals.at[part], sem_vals.at[k])

    table_copies = [
        pltpu.make_async_copy(mine_ref, table.at[pl.ds(0, half)], sem_table.at[0]),
        pltpu.make_async_copy(other_ref, table.at[pl.ds(half, half)], sem_table.at[1]),
    ]
    vals_copy(0).start()
    for copy in table_copies:
        copy.start()
    for k in range(1, chunks):
        @pl.when(k * CHUNK < count)
        def _(k=k):
            vals_copy(k).start()
    acc[...] = jnp.zeros_like(acc)
    for copy in table_copies:
        copy.wait()

    def group(g, _):
        slots = [g * GROUP + i for i in range(GROUP)]
        for i, s in enumerate(slots):
            place = pl.multiple_of(places_ref[s], tile)
            prods[i] = jnp.dot(vals[s], table[pl.ds(place, tile), :], preferred_element_type=jnp.float32)
        for i, s in enumerate(slots):
            row = pl.multiple_of(rows_ref[s], tile)
            acc[pl.ds(row, tile), :] += prods[i]
        return 0

    for k in range(chunks):
        @pl.when(k * CHUNK < count)
        def _(k=k):
            vals_copy(k).wait()
            left = jnp.minimum(count - k * CHUNK, CHUNK)
            lax.fori_loop(k * (CHUNK // GROUP), k * (CHUNK // GROUP) + (left + GROUP - 1) // GROUP, group, 0)
    out_ref[...] = acc[pl.ds(0, out_ref.shape[0]), :].astype(out_ref.dtype)


def aggregate(count, rows, places, mine, other, vals, out_rows):
    slots, tile, _ = vals.shape
    feat = mine.shape[1]
    smem = pl.BlockSpec(memory_space=pltpu.SMEM)
    hbm = pl.BlockSpec(memory_space=pl.ANY)
    return pl.pallas_call(
        aggregate_kernel,
        out_shape=jax.ShapeDtypeStruct((out_rows, feat), jnp.bfloat16),
        in_specs=[smem, smem, smem, hbm, hbm, hbm],
        out_specs=pl.BlockSpec(memory_space=pltpu.VMEM),
        scratch_shapes=[
            pltpu.VMEM((2 * mine.shape[0], feat), jnp.bfloat16),
            pltpu.VMEM((slots, tile, tile), jnp.bfloat16),
            pltpu.VMEM((out_rows + tile, feat), jnp.float32),
            pltpu.VMEM((GROUP, tile, feat), jnp.float32),
            pltpu.SemaphoreType.DMA((2,)),
            pltpu.SemaphoreType.DMA((slots // CHUNK,)),
        ],
        compiler_params=pltpu.CompilerParams(vmem_limit_bytes=32 * 2**20),
        cost_estimate=pl.CostEstimate(flops=2 * slots * tile * tile * feat, bytes_accessed=14 * 2**20, transcendentals=0),
        name="aggregate",
    )(count, rows, places, mine, other, vals)


def head_kernel(scale, own_ref, far_ref, weight_ref, labels_ref, logits_ref, grad_ref):
    total = far_ref[...].astype(jnp.float32)
    for k in range(own_ref.shape[0]):
        total += own_ref[k].astype(jnp.float32)
    upper = total.astype(jnp.bfloat16)
    lower = (total - upper.astype(jnp.float32)).astype(jnp.bfloat16)
    weight = weight_ref[...]
    logits = jnp.dot(upper, weight, preferred_element_type=jnp.float32)
    logits += jnp.dot(lower, weight, preferred_element_type=jnp.float32)
    logits_ref[...] = logits
    labels = labels_ref[...]
    classes = lax.broadcasted_iota(jnp.int32, logits.shape, 1)
    residual = logits - (labels == classes).astype(jnp.float32)
    residual = jnp.where(labels >= 0, residual, 0.0).astype(jnp.bfloat16)
    over_nodes = (((0,), (0,)), ((), ()))
    grad = lax.dot_general(upper, residual, over_nodes, preferred_element_type=jnp.float32)
    grad += lax.dot_general(lower, residual, over_nodes, preferred_element_type=jnp.float32)
    grad_ref[...] = grad * scale


def head(own, far, weight, labels, scale):
    rows, feat = far.shape
    classes = weight.shape[1]
    vmem = pl.BlockSpec(memory_space=pltpu.VMEM)
    return pl.pallas_call(
        lambda *refs: head_kernel(scale, *refs),
        out_shape=(
            jax.ShapeDtypeStruct((rows, classes), jnp.float32),
            jax.ShapeDtypeStruct((feat, classes), jnp.float32),
        ),
        in_specs=[vmem] * 4,
        out_specs=(vmem, vmem),
        compiler_params=pltpu.CompilerParams(vmem_limit_bytes=32 * 2**20),
        name="head",
    )(own, far, weight, labels)


def gather_features(features):
    plane = ("y", "zl")
    pieces = [features] + [shift(features, plane, -k) for k in range(1, lax.axis_size(plane))]
    mine = jnp.concatenate(pieces, 0)
    return mine, shift(mine, "core", 1)


def places_of(tile_cols, per_device, tile):
    device, part = tile_cols // per_device, tile_cols % per_device
    chip, core = device // 2, device % 2
    away = (chip - lax.axis_index(("y", "zl"))) % 16
    other = (core != lax.axis_index("core")).astype(jnp.int32)
    return (((other * 16 + away) * per_device) + part) * tile


def sum_everywhere(grad):
    core = lax.axis_index("core")
    half = grad.shape[0] // 2
    keep = lax.dynamic_slice_in_dim(grad, core * half, half, 0)
    give = lax.dynamic_slice_in_dim(grad, (1 - core) * half, half, 0)
    total = keep + shift(give, "core", 1)
    for axis in ("y", "zl", "x"):
        total = total + shift(total, axis, 1) + shift(total, axis, 2) + shift(total, axis, 3)
    total = total + shift(total, "zh", 1)
    rest = shift(total, "core", 1)
    return jnp.where(core == 0, jnp.concatenate([total, rest], 0), jnp.concatenate([rest, total], 0))


def local(features, weight, labels, tile_rows, tile_cols, tile_count, tile_vals):
    tile = tile_vals.shape[-1]
    slots = tile_vals.shape[2]
    vals = tile_vals.reshape(slots, tile, tile)
    count = tile_count.reshape(1)
    rows_out = features.shape[0] * lax.axis_size(COL)
    nodes = features.shape[0] * lax.axis_size(AXES)
    used = jnp.arange(slots, dtype=jnp.int32) < count
    rows = jnp.where(used, tile_rows.reshape(slots) * tile, rows_out)
    places = places_of(tile_cols.reshape(slots), features.shape[0] // tile, tile)

    mine, other = gather_features(features)
    part = aggregate(count, rows, places, mine, other, vals, rows_out)

    n_x = lax.axis_size("x")
    block = lax.all_to_all(part, "x", 0, 0, tiled=True).reshape(n_x, rows_out // n_x, -1)
    zh = lax.axis_index("zh")
    half = rows_out // n_x // 2
    give = lax.dynamic_slice_in_dim(block, (1 - zh) * half, half, 1)
    own = lax.dynamic_slice_in_dim(block, zh * half, half, 1)
    give = jnp.sum(give.astype(jnp.float32), 0).astype(jnp.bfloat16)
    far = shift(give, "zh", 1)
    logits, grad = head(own, far, weight, labels[:, None], 1.0 / math.sqrt(nodes))
    return logits, sum_everywhere(grad)


def solution(mesh):
    fine = Mesh(mesh.devices.reshape(SIZES), AXES)
    placed = (
        P(COL + ROW, None),
        P(),
        P(AXES),
        P(ROW, COL, None),
        P(ROW, COL, None),
        P(ROW, COL),
        P(ROW, COL, None, None, None),
    )
    return jax.shard_map(
        local, mesh=fine, in_specs=placed, out_specs=(P(AXES, None), P()), check_vma=False
    )
```

```python
import math

import jax
import jax.numpy as jnp
from jax import lax
from jax.experimental import pallas as pl
from jax.experimental.pallas import tpu as pltpu
from jax.sharding import Mesh, PartitionSpec as P

AXES = ("y", "zl", "core", "x", "zh")
SIZES = (4, 4, 2, 4, 2)
ROW = AXES[:3]
COL = AXES[3:]
GROUP = 8
CHUNK = 32


def shift(value, axes, step):
    n = lax.axis_size(axes)
    return lax.ppermute(value, axes, [(i, (i + step) % n) for i in range(n)])


def shift_z(value, step):
    n_lo, n_hi = lax.axis_size("zl"), lax.axis_size("zh")
    n = n_lo * n_hi
    at = lambda z: (z % n_lo) * n_hi + z // n_lo
    return lax.ppermute(value, ("zl", "zh"), [(at(z), at((z + step) % n)) for z in range(n)])


def fetch_kernel(count_ref, vals_ref, out_ref, sems):
    count = count_ref[0]

    def each(act):
        for k in range(vals_ref.shape[0] // CHUNK):
            @pl.when(k * CHUNK < count)
            def _(k=k):
                part = pl.ds(k * CHUNK, CHUNK)
                act(pltpu.make_async_copy(vals_ref.at[part], out_ref.at[part], sems.at[k]))

    each(lambda copy: copy.start())
    each(lambda copy: copy.wait())


def fetch(count, vals):
    return pl.pallas_call(
        fetch_kernel,
        out_shape=jax.ShapeDtypeStruct(vals.shape, vals.dtype),
        in_specs=[pl.BlockSpec(memory_space=pltpu.SMEM), pl.BlockSpec(memory_space=pltpu.HBM)],
        out_specs=pl.BlockSpec(memory_space=pltpu.VMEM),
        scratch_shapes=[pltpu.SemaphoreType.DMA((vals.shape[0] // CHUNK,))],
        compiler_params=pltpu.CompilerParams(vmem_limit_bytes=12 * 2**20),
        cost_estimate=pl.CostEstimate(flops=0, bytes_accessed=16 * 2**20, transcendentals=0),
        name="fetch",
    )(count, vals)


def aggregate_kernel(n_pieces, count_ref, rows_ref, places_ref, vals_ref, *refs):
    pieces, refs = refs[:n_pieces], refs[n_pieces:]
    own_ref, *away_refs = refs[:4]
    table, acc, prods, sem_table = refs[4:]
    tile = vals_ref.shape[-1]
    count = count_ref[0]

    table_copies, start = [], 0
    for i, piece in enumerate(pieces):
        rows = piece.shape[0]
        table_copies.append(pltpu.make_async_copy(piece, table.at[pl.ds(start, rows)], sem_table.at[i]))
        start += rows
    for copy in table_copies:
        copy.start()
    acc[...] = jnp.zeros_like(acc)
    for copy in table_copies:
        copy.wait()

    def group(g, _):
        slots = [g * GROUP + i for i in range(GROUP)]
        for i, s in enumerate(slots):
            place = pl.multiple_of(places_ref[s], tile)
            prods[i] = jnp.dot(vals_ref[s], table[pl.ds(place, tile), :], preferred_element_type=jnp.float32)
        for i, s in enumerate(slots):
            row = pl.multiple_of(rows_ref[s], tile)
            acc[pl.ds(row, tile), :] += prods[i]
        return 0

    lax.fori_loop(0, (count + GROUP - 1) // GROUP, group, 0)
    size = own_ref.shape[0]
    own_ref[...] = acc[pl.ds(0, size), :]
    for k, ref in enumerate(away_refs):
        ref[...] = acc[pl.ds((k + 1) * size, size), :].astype(ref.dtype)


def aggregate(count, rows, places, vals, pieces, out_rows):
    slots, tile, _ = vals.shape
    feat = pieces[0].shape[1]
    table_rows = sum(piece.shape[0] for piece in pieces)
    n_x = lax.axis_size("x")
    smem = pl.BlockSpec(memory_space=pltpu.SMEM)
    vmem = pl.BlockSpec(memory_space=pltpu.VMEM)
    shape = (out_rows // n_x, feat)
    return pl.pallas_call(
        lambda *refs: aggregate_kernel(len(pieces), *refs),
        out_shape=[jax.ShapeDtypeStruct(shape, jnp.float32)] + [jax.ShapeDtypeStruct(shape, jnp.bfloat16)] * (n_x - 1),
        in_specs=[smem, smem, smem, vmem] + [pl.BlockSpec(memory_space=pl.ANY)] * len(pieces),
        out_specs=[vmem] * n_x,
        scratch_shapes=[
            pltpu.VMEM((table_rows, feat), jnp.bfloat16),
            pltpu.VMEM((out_rows + tile, feat), jnp.float32),
            pltpu.VMEM((GROUP, tile, feat), jnp.float32),
            pltpu.SemaphoreType.DMA((len(pieces),)),
        ],
        compiler_params=pltpu.CompilerParams(vmem_limit_bytes=24 * 2**20),
        cost_estimate=pl.CostEstimate(flops=2 * slots * tile * tile * feat, bytes_accessed=14 * 2**20, transcendentals=0),
        name="aggregate",
    )(count, rows, places, vals, *pieces)


def head_kernel(scale, core_ref, own_ref, far_ref, *refs):
    *more_refs, weight_ref, labels_ref, logits_ref, keep_ref, give_ref = refs
    rows = far_ref.shape[0]
    total = own_ref[pl.ds(0, rows), :]
    for ref in more_refs:
        total += ref[pl.ds(0, rows), :].astype(jnp.float32)
    total += far_ref[...].astype(jnp.float32)
    upper = total.astype(jnp.bfloat16)
    lower = (total - upper.astype(jnp.float32)).astype(jnp.bfloat16)
    weight = weight_ref[...]
    by_feature = (((1,), (1,)), ((), ()))
    logits = lax.dot_general(weight, upper, by_feature, preferred_element_type=jnp.float32)
    logits += lax.dot_general(weight, lower, by_feature, preferred_element_type=jnp.float32)
    logits_ref[...] = logits
    labels = labels_ref[...]
    classes = lax.broadcasted_iota(jnp.int32, logits.shape, 0)
    residual = logits - (labels == classes).astype(jnp.float32)
    residual = jnp.where(labels >= 0, residual, 0.0).astype(jnp.bfloat16)
    grad = jnp.dot(residual, upper, preferred_element_type=jnp.float32)
    grad += jnp.dot(residual, lower, preferred_element_type=jnp.float32)
    grad = grad * scale
    half = keep_ref.shape[0]
    first, second = grad[:half], grad[half:]
    second = jnp.concatenate([second, jnp.zeros((2 * half - grad.shape[0], grad.shape[1]), grad.dtype)], 0)
    swap = core_ref[0] == 1
    keep_ref[...] = jnp.where(swap, second, first)
    give_ref[...] = jnp.where(swap, first, second)


def head(core, own, far, more, weight, labels, scale):
    rows, feat = far.shape
    classes = weight.shape[0]
    half = (classes + 15) // 16 * 8
    vmem = pl.BlockSpec(memory_space=pltpu.VMEM)
    return pl.pallas_call(
        lambda *refs: head_kernel(scale, *refs),
        out_shape=(
            jax.ShapeDtypeStruct((classes, rows), jnp.float32),
            jax.ShapeDtypeStruct((half, feat), jnp.float32),
            jax.ShapeDtypeStruct((half, feat), jnp.float32),
        ),
        in_specs=[pl.BlockSpec(memory_space=pltpu.SMEM)] + [vmem] * (4 + len(more)),
        out_specs=(vmem, vmem, vmem),
        compiler_params=pltpu.CompilerParams(vmem_limit_bytes=32 * 2**20),
        name="head",
    )(core, own, far, *more, weight, labels)


def gather_features(features):
    by_z = jnp.concatenate([features] + [shift(features, "zl", -k) for k in (1, 2, 3)], 0)
    opposite = shift(features, "y", 2)
    opposite = jnp.concatenate([opposite] + [shift(opposite, "zl", -k) for k in (1, 2, 3)], 0)
    mine = [by_z, shift(by_z, "y", -1), opposite, shift(by_z, "y", 1)]
    return mine + [shift(piece, "core", 1) for piece in mine]


def places_of(tile_cols, per_device, tile):
    device, part = tile_cols // per_device, tile_cols % per_device
    y, z, core = device // 8, device // 2 % 4, device % 2
    y = (y - lax.axis_index("y")) % 4
    z = (z - lax.axis_index("zl")) % 4
    core = (core - lax.axis_index("core")) % 2
    return (((core * 4 + y) * 4 + z) * per_device + part) * tile


def rows_of(tile_rows, per_device, tile):
    device, part = tile_rows // per_device, tile_rows % per_device
    x, zh = device // 2, device % 2
    x = (x - lax.axis_index("x")) % 4
    zh = (zh - lax.axis_index("zh")) % 2
    return ((x * 2 + zh) * per_device + part) * tile


def sum_everywhere(keep, give, core, classes):
    total = keep + shift(give, "core", 1)
    for axis in ("y", "x"):
        total = total + shift(total, axis, 1) + shift(total, axis, 2) + shift(total, axis, 3)
    total = total + shift(total, "zh", 1)
    total = total + shift_z(total, 1) + shift_z(total, 2) + shift_z(total, -1)
    rest = shift(total, "core", 1)
    swap = core == 1
    return jnp.concatenate([jnp.where(swap, rest, total), jnp.where(swap, total, rest)], 0)[:classes]


def local(features, weight, labels, tile_rows, tile_cols, tile_count, tile_vals):
    tile = tile_vals.shape[-1]
    slots = tile_vals.shape[2]
    classes = weight.shape[1]
    nodes, feat = features.shape
    vals = tile_vals.reshape(slots, tile, tile)
    count = tile_count.reshape(1)
    out_rows = nodes * lax.axis_size(COL)
    used = jnp.arange(slots, dtype=jnp.int32) < count
    rows = jnp.where(used, rows_of(tile_rows.reshape(slots), nodes // tile, tile), out_rows)
    places = places_of(tile_cols.reshape(slots), nodes // tile, tile)
    core = lax.axis_index("core").astype(jnp.int32)

    pieces = gather_features(features)
    own, *away = aggregate(count, rows, places, fetch(count, vals), pieces, out_rows)
    more = [shift(part, "x", k + 1) for k, part in enumerate(away)]
    give = own[nodes:] + sum(part[nodes:].astype(jnp.float32) for part in more)
    far = shift(give.astype(jnp.bfloat16), "zh", 1)
    scale = 1.0 / math.sqrt(nodes * lax.axis_size(AXES))
    logits, keep, give = head(core.reshape(1), own, far, more, weight.T, labels.reshape(1, nodes), scale)
    return logits.T, sum_everywhere(keep, give, core, classes).T


def solution(mesh):
    fine = Mesh(mesh.devices.reshape(SIZES), AXES)
    placed = (
        P(COL + ROW, None),
        P(),
        P(AXES),
        P(ROW, COL, None),
        P(ROW, COL, None),
        P(ROW, COL),
        P(ROW, COL, None, None, None),
    )
    return jax.shard_map(
        local, mesh=fine, in_specs=placed, out_specs=(P(AXES, None), P()), check_vma=False
    )
```

```python
import functools
import math

import jax
import jax.numpy as jnp
from jax import lax
from jax.experimental import pallas as pl
from jax.experimental.pallas import tpu as pltpu
from jax.sharding import Mesh, PartitionSpec as P

AXES = ("y", "zl", "core", "x", "zh")
SIZES = (4, 4, 2, 4, 2)
ROW = AXES[:3]
COL = AXES[3:]
GROUP = 8


def shift(value, axes, step):
    n = lax.axis_size(axes)
    return lax.ppermute(value, axes, [(i, (i + step) % n) for i in range(n)])


def shift_z(value, step):
    n_lo, n_hi = lax.axis_size("zl"), lax.axis_size("zh")
    n = n_lo * n_hi
    at = lambda z: (z % n_lo) * n_hi + z // n_lo
    return lax.ppermute(value, ("zl", "zh"), [(at(z), at((z + step) % n)) for z in range(n)])


def plan_kernel(per_device, tile, place_ref, rows_ref, cols_ref, plan_ref):
    y0, z0, core0, x0, zh0, count = (place_ref[i] for i in range(6))
    slots = rows_ref.shape[1]
    slot = lax.broadcasted_iota(jnp.int32, (1, slots), 1)
    device, part = rows_ref[...] // per_device, rows_ref[...] % per_device
    row = (device // 2 - x0) % 4 * per_device + part
    far = (device % 2 - zh0) % 2 == 1
    device, part = cols_ref[...] // per_device, cols_ref[...] % per_device
    place = (device % 2 - core0) % 2 * 4 + (device // 8 - y0) % 4
    place = (place * 4 + (device // 2 % 4 - z0) % 4) * per_device + part
    used = slot < count
    before = lax.broadcasted_iota(jnp.int32, (slots, slots), 0) <= lax.broadcasted_iota(jnp.int32, (slots, slots), 1)
    before = before.astype(jnp.bfloat16)
    listed = lax.broadcasted_iota(jnp.int32, (slots, slots), 0)
    blank = jnp.zeros((5, slots), jnp.float32)
    values = jnp.concatenate([v.astype(jnp.float32) for v in (slot, row, place)] + [blank], 0).astype(jnp.bfloat16)
    by_slot = (((1,), (1,)), ((), ()))
    for k, member in enumerate((used & far, used & jnp.logical_not(far))):
        marks = jnp.broadcast_to(member.astype(jnp.float32), (8, slots)).astype(jnp.bfloat16)
        rank = jnp.dot(marks, before, preferred_element_type=jnp.float32)[:1].astype(jnp.int32)
        size = jnp.max(rank, axis=1, keepdims=True)
        rank = jnp.where(member, rank - 1, -1)
        picks = (listed == rank).astype(jnp.float32).astype(jnp.bfloat16)
        chosen = lax.dot_general(values, picks, by_slot, preferred_element_type=jnp.float32).astype(jnp.int32)
        filled = slot < size
        plan_ref[pl.ds(4 * k, 1), :] = chosen[0:1]
        plan_ref[pl.ds(4 * k + 1, 1), :] = jnp.where(filled, chosen[1:2], 4 * per_device) * tile
        plan_ref[pl.ds(4 * k + 2, 1), :] = chosen[2:3] * tile
        plan_ref[pl.ds(4 * k + 3, 1), :] = jnp.broadcast_to(size, (1, slots))


def plan(tile_rows, tile_cols, count, per_device, tile):
    slots = tile_rows.shape[1]
    vmem = pl.BlockSpec(memory_space=pltpu.VMEM)
    place = jnp.stack([lax.axis_index(axis) for axis in AXES] + [count]).astype(jnp.int32)
    return pl.pallas_call(
        lambda *refs: plan_kernel(per_device, tile, *refs),
        out_shape=jax.ShapeDtypeStruct((8, slots), jnp.int32),
        in_specs=[pl.BlockSpec(memory_space=pltpu.SMEM), vmem, vmem],
        out_specs=vmem,
        name="plan",
    )(place, tile_rows, tile_cols)


def sum_tiles(part, plan_ref, vals_ref, table_ref, own_ref, away_refs, vals, acc, prods, sems, beside=None):
    tile = vals.shape[-1]
    groups = (plan_ref[4 * part + 3, 0] + GROUP - 1) // GROUP

    def fetch(g, _):
        for i in range(GROUP):
            s = g * GROUP + i
            pltpu.make_async_copy(vals_ref.at[plan_ref[4 * part, s]], vals.at[s], sems.at[g]).start()
        return 0

    lax.fori_loop(0, groups, fetch, 0)
    acc[...] = jnp.zeros_like(acc)
    if beside is not None:
        beside()

    def group(g, _):
        here = pl.ds(g * GROUP, GROUP)
        pltpu.make_async_copy(vals_ref.at[pl.ds(0, GROUP)], vals.at[here], sems.at[g]).wait()
        slots = [g * GROUP + i for i in range(GROUP)]
        for i, s in enumerate(slots):
            place = pl.multiple_of(plan_ref[4 * part + 2, s], tile)
            prods[i] = jnp.dot(vals[s], table_ref[pl.ds(place, tile), :], preferred_element_type=jnp.float32)
        for i, s in enumerate(slots):
            row = pl.multiple_of(plan_ref[4 * part + 1, s], tile)
            acc[pl.ds(row, tile), :] += prods[i]
        return 0

    lax.fori_loop(0, groups, group, 0)
    size = own_ref.shape[0]
    own_ref[...] = acc[pl.ds(0, size), :]
    for k, ref in enumerate(away_refs):
        ref[...] = acc[pl.ds((k + 1) * size, size), :].astype(ref.dtype)


def far_kernel(n_pieces, plan_ref, vals_ref, *refs):
    pieces, refs = refs[:n_pieces], refs[n_pieces:]
    table_ref, own_ref, *away_refs = refs[:5]
    vals, acc, prods, sems, sem_table = refs[5:]
    copies, start = [], 0
    for i, piece in enumerate(pieces):
        rows = piece.shape[0]
        copies.append(pltpu.make_async_copy(piece, table_ref.at[pl.ds(start, rows)], sem_table.at[i]))
        copies[-1].start()
        start += rows
    sum_tiles(0, plan_ref, vals_ref, table_ref, own_ref, away_refs, vals, acc, prods, sems,
              lambda: [copy.wait() for copy in copies])


def near_kernel(plan_ref, vals_ref, table_ref, own_ref, *refs):
    sum_tiles(1, plan_ref, vals_ref, table_ref, own_ref, refs[:3], *refs[3:])


def aggregate(kernel, plan, vals, pieces, out_rows, with_table):
    slots, tile, _ = vals.shape
    feat = pieces[0].shape[1]
    table_rows = sum(piece.shape[0] for piece in pieces)
    n_x = lax.axis_size("x")
    vmem = pl.BlockSpec(memory_space=pltpu.VMEM)
    shape = (out_rows // n_x, feat)
    out = [jax.ShapeDtypeStruct(shape, jnp.float32)] + [jax.ShapeDtypeStruct(shape, jnp.bfloat16)] * (n_x - 1)
    scratch = [
        pltpu.VMEM((slots, tile, tile), jnp.bfloat16),
        pltpu.VMEM((out_rows + tile, feat), jnp.float32),
        pltpu.VMEM((GROUP, tile, feat), jnp.float32),
        pltpu.SemaphoreType.DMA((slots // GROUP,)),
    ]
    if with_table:
        out = [jax.ShapeDtypeStruct((table_rows, feat), jnp.bfloat16)] + out
        scratch.append(pltpu.SemaphoreType.DMA((len(pieces),)))
    near = pl.BlockSpec(memory_space=pl.ANY) if with_table else vmem
    return pl.pallas_call(
        kernel,
        out_shape=out,
        in_specs=[pl.BlockSpec(memory_space=pltpu.SMEM), pl.BlockSpec(memory_space=pltpu.HBM)] + [near] * len(pieces),
        out_specs=[vmem] * len(out),
        scratch_shapes=scratch,
        compiler_params=pltpu.CompilerParams(vmem_limit_bytes=24 * 2**20),
        cost_estimate=pl.CostEstimate(flops=slots * tile * tile * feat, bytes_accessed=8 * 2**20, transcendentals=0),
        name="far_rows" if with_table else "near_rows",
    )(plan, vals, *pieces)


def head_kernel(scale, core_ref, own_ref, far_ref, *refs):
    *more_refs, weight_ref, labels_ref, logits_ref, keep_ref, give_ref = refs
    total = own_ref[...]
    for ref in more_refs:
        total += ref[...].astype(jnp.float32)
    total += far_ref[...].astype(jnp.float32)
    upper = total.astype(jnp.bfloat16)
    lower = (total - upper.astype(jnp.float32)).astype(jnp.bfloat16)
    weight = weight_ref[...]
    by_feature = (((1,), (1,)), ((), ()))
    logits = lax.dot_general(weight, upper, by_feature, preferred_element_type=jnp.float32)
    logits += lax.dot_general(weight, lower, by_feature, preferred_element_type=jnp.float32)
    logits_ref[...] = logits
    labels = labels_ref[...]
    classes = lax.broadcasted_iota(jnp.int32, logits.shape, 0)
    residual = logits - (labels == classes).astype(jnp.float32)
    residual = jnp.where(labels >= 0, residual, 0.0).astype(jnp.bfloat16)
    grad = jnp.dot(residual, upper, preferred_element_type=jnp.float32)
    grad += jnp.dot(residual, lower, preferred_element_type=jnp.float32)
    grad = grad * scale
    half = keep_ref.shape[0]
    first, second = grad[:half], grad[half:]
    second = jnp.concatenate([second, jnp.zeros((2 * half - grad.shape[0], grad.shape[1]), grad.dtype)], 0)
    swap = core_ref[0] == 1
    keep_ref[...] = jnp.where(swap, second, first)
    give_ref[...] = jnp.where(swap, first, second)


def head(core, own, far, more, weight, labels, scale):
    rows, feat = far.shape
    classes = weight.shape[0]
    half = (classes + 15) // 16 * 8
    vmem = pl.BlockSpec(memory_space=pltpu.VMEM)
    return pl.pallas_call(
        lambda *refs: head_kernel(scale, *refs),
        out_shape=(
            jax.ShapeDtypeStruct((classes, rows), jnp.float32),
            jax.ShapeDtypeStruct((half, feat), jnp.float32),
            jax.ShapeDtypeStruct((half, feat), jnp.float32),
        ),
        in_specs=[pl.BlockSpec(memory_space=pltpu.SMEM)] + [vmem] * (4 + len(more)),
        out_specs=(vmem, vmem, vmem),
        compiler_params=pltpu.CompilerParams(vmem_limit_bytes=32 * 2**20),
        name="head",
    )(core, own, far, *more, weight, labels)


def gather_features(features):
    by_z = jnp.concatenate([features] + [shift(features, "zl", -k) for k in (1, 2, 3)], 0)
    opposite = shift(features, "y", 2)
    opposite = jnp.concatenate([opposite] + [shift(opposite, "zl", -k) for k in (1, 2, 3)], 0)
    mine = [by_z, shift(by_z, "y", -1), opposite, shift(by_z, "y", 1)]
    return mine + [shift(piece, "core", 1) for piece in mine]


def sum_everywhere(keep, give, core, classes):
    total = keep + shift(give, "core", 1)
    for axis in ("y", "x"):
        total = total + shift(total, axis, 1) + shift(total, axis, 2) + shift(total, axis, 3)
    total = total + shift(total, "zh", 1)
    total = total + shift_z(total, 1) + shift_z(total, 2) + shift_z(total, -1)
    rest = shift(total, "core", 1)
    swap = core == 1
    return jnp.concatenate([jnp.where(swap, rest, total), jnp.where(swap, total, rest)], 0)[:classes]


def local(features, weight, labels, tile_rows, tile_cols, tile_count, tile_vals):
    tile = tile_vals.shape[-1]
    slots = tile_vals.shape[2]
    classes = weight.shape[1]
    nodes = features.shape[0]
    vals = pltpu.with_memory_space_constraint(tile_vals.reshape(slots, tile, tile), pltpu.HBM)
    out_rows = nodes * lax.axis_size("x")
    core = lax.axis_index("core").astype(jnp.int32)
    lists = plan(
        tile_rows.reshape(1, slots), tile_cols.reshape(1, slots), tile_count.reshape(()), nodes // tile, tile
    )

    pieces = gather_features(features)
    table, own, *away = aggregate(functools.partial(far_kernel, len(pieces)), lists, vals, pieces, out_rows, True)
    give = own + sum(shift(away[k], "x", k + 1).astype(jnp.float32) for k in (1, 0, 2))
    own, *away = aggregate(near_kernel, lists, vals, [table], out_rows, False)
    more = [shift(away[k], "x", k + 1) for k in (1, 0, 2)]
    far = shift(give.astype(jnp.bfloat16), "zh", 1)
    scale = 1.0 / math.sqrt(nodes * lax.axis_size(AXES))
    logits, keep, give = head(core.reshape(1), own, far, more, weight.T, labels.reshape(1, nodes), scale)
    return logits.T, sum_everywhere(keep, give, core, classes).T


def solution(mesh):
    fine = Mesh(mesh.devices.reshape(SIZES), AXES)
    placed = (
        P(COL + ROW, None),
        P(),
        P(AXES),
        P(ROW, COL, None),
        P(ROW, COL, None),
        P(ROW, COL),
        P(ROW, COL, None, None, None),
    )
    return jax.shard_map(
        local, mesh=fine, in_specs=placed, out_specs=(P(AXES, None), P()), check_vma=False
    )
```

```python
import functools
import math

import jax
import jax.numpy as jnp
from jax import lax
from jax.experimental import pallas as pl
from jax.experimental.pallas import tpu as pltpu
from jax.sharding import Mesh, PartitionSpec as P

AXES = ("y", "zl", "core", "x", "zh")
SIZES = (4, 4, 2, 4, 2)
ROW = AXES[:3]
COL = AXES[3:]
GROUP = 32
CHUNK = 32


def shift(value, axes, step):
    n = lax.axis_size(axes)
    return lax.ppermute(value, axes, [(i, (i + step) % n) for i in range(n)])


def shift_z(value, step):
    n_lo, n_hi = lax.axis_size("zl"), lax.axis_size("zh")
    n = n_lo * n_hi
    at = lambda z: (z % n_lo) * n_hi + z // n_lo
    return lax.ppermute(value, ("zl", "zh"), [(at(z), at((z + step) % n)) for z in range(n)])


def plan_kernel(per_device, tile, place_ref, rows_ref, cols_ref, plan_ref):
    y0, z0, core0, x0, zh0, count = (place_ref[i] for i in range(6))
    slots = rows_ref.shape[1]
    slot = lax.broadcasted_iota(jnp.int32, (1, slots), 1)
    device, part = rows_ref[...] // per_device, rows_ref[...] % per_device
    row = (device // 2 - x0) % 4 * per_device + part
    far = (device % 2 - zh0) % 2 == 1
    device, part = cols_ref[...] // per_device, cols_ref[...] % per_device
    place = (device % 2 - core0) % 2 * 4 + (device // 8 - y0) % 4
    place = (place * 4 + (device // 2 % 4 - z0) % 4) * per_device + part
    used = slot < count
    before = lax.broadcasted_iota(jnp.int32, (slots, slots), 0) <= lax.broadcasted_iota(jnp.int32, (slots, slots), 1)
    before = before.astype(jnp.bfloat16)
    listed = lax.broadcasted_iota(jnp.int32, (slots, slots), 0)
    blank = jnp.zeros((5, slots), jnp.float32)
    values = jnp.concatenate([v.astype(jnp.float32) for v in (slot, row, place)] + [blank], 0).astype(jnp.bfloat16)
    by_slot = (((1,), (1,)), ((), ()))
    for k, member in enumerate((used & far, used & jnp.logical_not(far))):
        marks = jnp.broadcast_to(member.astype(jnp.float32), (8, slots)).astype(jnp.bfloat16)
        rank = jnp.dot(marks, before, preferred_element_type=jnp.float32)[:1].astype(jnp.int32)
        size = jnp.max(rank, axis=1, keepdims=True)
        rank = jnp.where(member, rank - 1, -1)
        picks = (listed == rank).astype(jnp.float32).astype(jnp.bfloat16)
        chosen = lax.dot_general(values, picks, by_slot, preferred_element_type=jnp.float32).astype(jnp.int32)
        filled = slot < size
        plan_ref[pl.ds(4 * k, 1), :] = chosen[0:1]
        plan_ref[pl.ds(4 * k + 1, 1), :] = jnp.where(filled, chosen[1:2], 4 * per_device) * tile
        plan_ref[pl.ds(4 * k + 2, 1), :] = chosen[2:3] * tile
        plan_ref[pl.ds(4 * k + 3, 1), :] = jnp.broadcast_to(size, (1, slots))


def plan(tile_rows, tile_cols, count, per_device, tile):
    slots = tile_rows.shape[1]
    vmem = pl.BlockSpec(memory_space=pltpu.VMEM)
    place = jnp.stack([lax.axis_index(axis) for axis in AXES] + [count]).astype(jnp.int32)
    return pl.pallas_call(
        lambda *refs: plan_kernel(per_device, tile, *refs),
        out_shape=jax.ShapeDtypeStruct((8, slots), jnp.int32),
        in_specs=[pl.BlockSpec(memory_space=pltpu.SMEM), vmem, vmem],
        out_specs=vmem,
        name="plan",
    )(place, tile_rows, tile_cols)


def fetch_kernel(plan_ref, vals_ref, out_ref, token_ref, sems):
    count = plan_ref[3, 0] + plan_ref[7, 0]

    def each(act):
        for k in range(vals_ref.shape[0] // CHUNK):
            @pl.when(k * CHUNK < count)
            def _(k=k):
                part = pl.ds(k * CHUNK, CHUNK)
                act(pltpu.make_async_copy(vals_ref.at[part], out_ref.at[part], sems.at[k]))

    each(lambda copy: copy.start())
    each(lambda copy: copy.wait())
    token_ref[0] = count


def fetch(plan, vals):
    smem = pl.BlockSpec(memory_space=pltpu.SMEM)
    return pl.pallas_call(
        fetch_kernel,
        out_shape=(jax.ShapeDtypeStruct(vals.shape, vals.dtype), jax.ShapeDtypeStruct((1,), jnp.int32)),
        in_specs=[smem, pl.BlockSpec(memory_space=pltpu.HBM)],
        out_specs=(pl.BlockSpec(memory_space=pltpu.VMEM), smem),
        scratch_shapes=[pltpu.SemaphoreType.DMA((vals.shape[0] // CHUNK,))],
        compiler_params=pltpu.CompilerParams(vmem_limit_bytes=12 * 2**20),
        cost_estimate=pl.CostEstimate(flops=0, bytes_accessed=16 * 2**20, transcendentals=0),
        name="fetch",
    )(plan, vals)


def sum_tiles(part, plan_ref, vals_ref, table_ref, own_ref, away_refs, acc, prods):
    tile = vals_ref.shape[-1]

    def group(g, _):
        entries = [g * GROUP + i for i in range(GROUP)]
        for i, s in enumerate(entries):
            place = pl.multiple_of(plan_ref[4 * part + 2, s], tile)
            prods[i] = jnp.dot(
                vals_ref[plan_ref[4 * part, s]], table_ref[pl.ds(place, tile), :], preferred_element_type=jnp.float32
            )
        for i, s in enumerate(entries):
            row = pl.multiple_of(plan_ref[4 * part + 1, s], tile)
            acc[pl.ds(row, tile), :] += prods[i]
        return 0

    lax.fori_loop(0, (plan_ref[4 * part + 3, 0] + GROUP - 1) // GROUP, group, 0)
    size = own_ref.shape[0]
    own_ref[...] = acc[pl.ds(0, size), :]
    for k, ref in enumerate(away_refs):
        ref[...] = acc[pl.ds((k + 1) * size, size), :].astype(ref.dtype)


def far_kernel(n_pieces, plan_ref, vals_ref, *refs):
    pieces, refs = refs[:n_pieces], refs[n_pieces:]
    table_ref, own_ref, *away_refs = refs[:5]
    acc, prods, sem_table = refs[5:]
    copies, start = [], 0
    for i, piece in enumerate(pieces):
        rows = piece.shape[0]
        copies.append(pltpu.make_async_copy(piece, table_ref.at[pl.ds(start, rows)], sem_table.at[i]))
        copies[-1].start()
        start += rows
    acc[...] = jnp.zeros_like(acc)
    for copy in copies:
        copy.wait()
    sum_tiles(0, plan_ref, vals_ref, table_ref, own_ref, away_refs, acc, prods)


def near_kernel(plan_ref, vals_ref, table_ref, own_ref, *refs):
    acc, prods = refs[3:]
    acc[...] = jnp.zeros_like(acc)
    sum_tiles(1, plan_ref, vals_ref, table_ref, own_ref, refs[:3], acc, prods)


def aggregate(kernel, plan, vals, pieces, out_rows, with_table):
    slots, tile, _ = vals.shape
    feat = pieces[0].shape[1]
    table_rows = sum(piece.shape[0] for piece in pieces)
    n_x = lax.axis_size("x")
    vmem = pl.BlockSpec(memory_space=pltpu.VMEM)
    shape = (out_rows // n_x, feat)
    out = [jax.ShapeDtypeStruct(shape, jnp.float32)] + [jax.ShapeDtypeStruct(shape, jnp.bfloat16)] * (n_x - 1)
    scratch = [
        pltpu.VMEM((out_rows + tile, feat), jnp.float32),
        pltpu.VMEM((GROUP, tile, feat), jnp.float32),
    ]
    if with_table:
        out = [jax.ShapeDtypeStruct((table_rows, feat), jnp.bfloat16)] + out
        scratch.append(pltpu.SemaphoreType.DMA((len(pieces),)))
    near = pl.BlockSpec(memory_space=pl.ANY) if with_table else vmem
    return pl.pallas_call(
        kernel,
        out_shape=out,
        in_specs=[pl.BlockSpec(memory_space=pltpu.SMEM), vmem] + [near] * len(pieces),
        out_specs=[vmem] * len(out),
        scratch_shapes=scratch,
        compiler_params=pltpu.CompilerParams(vmem_limit_bytes=20 * 2**20),
        cost_estimate=pl.CostEstimate(flops=slots * tile * tile * feat, bytes_accessed=8 * 2**20, transcendentals=0),
        name="far_rows" if with_table else "near_rows",
    )(plan, vals, *pieces)


def head_kernel(scale, core_ref, own_ref, far_ref, *refs):
    *more_refs, weight_ref, labels_ref, logits_ref, keep_ref, give_ref = refs
    total = own_ref[...]
    for ref in more_refs:
        total += ref[...].astype(jnp.float32)
    total += far_ref[...].astype(jnp.float32)
    upper = total.astype(jnp.bfloat16)
    lower = (total - upper.astype(jnp.float32)).astype(jnp.bfloat16)
    weight = weight_ref[...]
    by_feature = (((1,), (1,)), ((), ()))
    logits = lax.dot_general(weight, upper, by_feature, preferred_element_type=jnp.float32)
    logits += lax.dot_general(weight, lower, by_feature, preferred_element_type=jnp.float32)
    logits_ref[...] = logits
    labels = labels_ref[...]
    classes = lax.broadcasted_iota(jnp.int32, logits.shape, 0)
    residual = logits - (labels == classes).astype(jnp.float32)
    residual = jnp.where(labels >= 0, residual, 0.0).astype(jnp.bfloat16)
    grad = jnp.dot(residual, upper, preferred_element_type=jnp.float32)
    grad += jnp.dot(residual, lower, preferred_element_type=jnp.float32)
    grad = grad * scale
    half = keep_ref.shape[0]
    first, second = grad[:half], grad[half:]
    second = jnp.concatenate([second, jnp.zeros((2 * half - grad.shape[0], grad.shape[1]), grad.dtype)], 0)
    swap = core_ref[0] == 1
    keep_ref[...] = jnp.where(swap, second, first)
    give_ref[...] = jnp.where(swap, first, second)


def head(core, own, far, more, weight, labels, scale):
    rows, feat = far.shape
    classes = weight.shape[0]
    half = (classes + 15) // 16 * 8
    vmem = pl.BlockSpec(memory_space=pltpu.VMEM)
    return pl.pallas_call(
        lambda *refs: head_kernel(scale, *refs),
        out_shape=(
            jax.ShapeDtypeStruct((classes, rows), jnp.float32),
            jax.ShapeDtypeStruct((half, feat), jnp.float32),
            jax.ShapeDtypeStruct((half, feat), jnp.float32),
        ),
        in_specs=[pl.BlockSpec(memory_space=pltpu.SMEM)] + [vmem] * (4 + len(more)),
        out_specs=(vmem, vmem, vmem),
        compiler_params=pltpu.CompilerParams(vmem_limit_bytes=32 * 2**20),
        name="head",
    )(core, own, far, *more, weight, labels)


def after(value, token):
    return jnp.where(token[0] < 0, jnp.zeros_like(value), value)


def gather_features(features, token):
    by_z = jnp.concatenate([features] + [shift(features, "zl", -k) for k in (1, 2, 3)], 0)
    opposite = after(shift(features, "y", 2), token)
    opposite = jnp.concatenate([opposite] + [shift(opposite, "zl", -k) for k in (1, 2, 3)], 0)
    mine = [by_z, shift(by_z, "y", -1), opposite, shift(by_z, "y", 1)]
    return mine + [shift(piece, "core", 1) for piece in mine]


def sum_everywhere(keep, give, core, classes):
    total = keep + shift(give, "core", 1)
    for axis in ("y", "x"):
        total = (total + shift(total, axis, 2)) + (shift(total, axis, 1) + shift(total, axis, 3))
    total = total + shift(total, "zh", 1)
    total = (total + shift_z(total, 2)) + (shift_z(total, 1) + shift_z(total, -1))
    rest = shift(total, "core", 1)
    swap = core == 1
    return jnp.concatenate([jnp.where(swap, rest, total), jnp.where(swap, total, rest)], 0)[:classes]


def local(features, weight, labels, tile_rows, tile_cols, tile_count, tile_vals):
    tile = tile_vals.shape[-1]
    slots = tile_vals.shape[2]
    classes = weight.shape[1]
    nodes = features.shape[0]
    vals = pltpu.with_memory_space_constraint(tile_vals.reshape(slots, tile, tile), pltpu.HBM)
    out_rows = nodes * lax.axis_size("x")
    core = lax.axis_index("core").astype(jnp.int32)
    lists = plan(
        tile_rows.reshape(1, slots), tile_cols.reshape(1, slots), tile_count.reshape(()), nodes // tile, tile
    )

    vals, token = fetch(lists, vals)
    pieces = gather_features(features, token)
    table, own, *away = aggregate(functools.partial(far_kernel, len(pieces)), lists, vals, pieces, out_rows, True)
    give = own + sum(shift(away[k], "x", k + 1).astype(jnp.float32) for k in (1, 0, 2))
    own, *away = aggregate(near_kernel, lists, vals, [table], out_rows, False)
    more = [shift(away[k], "x", k + 1) for k in (1, 0, 2)]
    far = shift(give.astype(jnp.bfloat16), "zh", 1)
    scale = 1.0 / math.sqrt(nodes * lax.axis_size(AXES))
    logits, keep, give = head(core.reshape(1), own, far, more, weight.T, labels.reshape(1, nodes), scale)
    return logits.T, sum_everywhere(keep, give, core, classes).T


def solution(mesh):
    fine = Mesh(mesh.devices.reshape(SIZES), AXES)
    placed = (
        P(COL + ROW, None),
        P(),
        P(AXES),
        P(ROW, COL, None),
        P(ROW, COL, None),
        P(ROW, COL),
        P(ROW, COL, None, None, None),
    )
    return jax.shard_map(
        local, mesh=fine, in_specs=placed, out_specs=(P(AXES, None), P()), check_vma=False
    )
```

```python
import functools
import math

import jax
import jax.numpy as jnp
from jax import lax
from jax.experimental import pallas as pl
from jax.experimental.pallas import tpu as pltpu
from jax.sharding import Mesh, PartitionSpec as P

AXES = ("y", "zl", "core", "x", "zh")
SIZES = (4, 4, 2, 4, 2)
ROW = AXES[:3]
COL = AXES[3:]
GROUP = 32
CHUNK = 32


def shift(value, axes, step):
    n = lax.axis_size(axes)
    return lax.ppermute(value, axes, [(i, (i + step) % n) for i in range(n)])


def shift_z(value, step):
    n_lo, n_hi = lax.axis_size("zl"), lax.axis_size("zh")
    n = n_lo * n_hi
    at = lambda z: (z % n_lo) * n_hi + z // n_lo
    return lax.ppermute(value, ("zl", "zh"), [(at(z), at((z + step) % n)) for z in range(n)])


def plan_kernel(per_device, tile, count_ref, rows_ref, cols_ref, plan_ref):
    y0, z0, core0, x0, zh0 = (lax.axis_index(axis) for axis in AXES)
    count = count_ref[0]
    slots = rows_ref.shape[1]
    slot = lax.broadcasted_iota(jnp.int32, (1, slots), 1)
    device, part = rows_ref[...] // per_device, rows_ref[...] % per_device
    row = (device // 2 - x0) % 4 * per_device + part
    far = (device % 2 - zh0) % 2 == 1
    device, part = cols_ref[...] // per_device, cols_ref[...] % per_device
    place = (device % 2 - core0) % 2 * 4 + (device // 8 - y0) % 4
    place = (place * 4 + (device // 2 % 4 - z0) % 4) * per_device + part
    used = slot < count
    before = lax.broadcasted_iota(jnp.int32, (slots, slots), 0) <= lax.broadcasted_iota(jnp.int32, (slots, slots), 1)
    before = before.astype(jnp.bfloat16)
    listed = lax.broadcasted_iota(jnp.int32, (slots, slots), 0)
    blank = jnp.zeros((5, slots), jnp.float32)
    values = jnp.concatenate([v.astype(jnp.float32) for v in (slot, row, place)] + [blank], 0).astype(jnp.bfloat16)
    by_slot = (((1,), (1,)), ((), ()))
    for k, member in enumerate((used & far, used & jnp.logical_not(far))):
        marks = jnp.broadcast_to(member.astype(jnp.float32), (8, slots)).astype(jnp.bfloat16)
        rank = jnp.dot(marks, before, preferred_element_type=jnp.float32)[:1].astype(jnp.int32)
        size = jnp.max(rank, axis=1, keepdims=True)
        rank = jnp.where(member, rank - 1, -1)
        picks = (listed == rank).astype(jnp.float32).astype(jnp.bfloat16)
        chosen = lax.dot_general(values, picks, by_slot, preferred_element_type=jnp.float32).astype(jnp.int32)
        filled = slot < size
        plan_ref[pl.ds(4 * k, 1), :] = chosen[0:1]
        plan_ref[pl.ds(4 * k + 1, 1), :] = jnp.where(filled, chosen[1:2], 4 * per_device) * tile
        plan_ref[pl.ds(4 * k + 2, 1), :] = chosen[2:3] * tile
        plan_ref[pl.ds(4 * k + 3, 1), :] = jnp.broadcast_to(size, (1, slots))


def plan(tile_rows, tile_cols, count, per_device, tile):
    slots = tile_rows.shape[1]
    vmem = pl.BlockSpec(memory_space=pltpu.VMEM)
    return pl.pallas_call(
        lambda *refs: plan_kernel(per_device, tile, *refs),
        out_shape=jax.ShapeDtypeStruct((8, slots), jnp.int32),
        in_specs=[pl.BlockSpec(memory_space=pltpu.SMEM), vmem, vmem],
        out_specs=vmem,
        name="plan",
    )(count, tile_rows, tile_cols)


def fetch_kernel(plan_ref, vals_ref, out_ref, token_ref, sems):
    count = plan_ref[3, 0] + plan_ref[7, 0]

    def each(act):
        for k in range(vals_ref.shape[0] // CHUNK):
            @pl.when(k * CHUNK < count)
            def _(k=k):
                part = pl.ds(k * CHUNK, CHUNK)
                act(pltpu.make_async_copy(vals_ref.at[part], out_ref.at[part], sems.at[k]))

    each(lambda copy: copy.start())
    each(lambda copy: copy.wait())
    token_ref[0] = count


def fetch(plan, vals):
    smem = pl.BlockSpec(memory_space=pltpu.SMEM)
    return pl.pallas_call(
        fetch_kernel,
        out_shape=(jax.ShapeDtypeStruct(vals.shape, vals.dtype), jax.ShapeDtypeStruct((1,), jnp.int32)),
        in_specs=[smem, pl.BlockSpec(memory_space=pltpu.HBM)],
        out_specs=(pl.BlockSpec(memory_space=pltpu.VMEM), smem),
        scratch_shapes=[pltpu.SemaphoreType.DMA((vals.shape[0] // CHUNK,))],
        compiler_params=pltpu.CompilerParams(vmem_limit_bytes=12 * 2**20),
        cost_estimate=pl.CostEstimate(flops=0, bytes_accessed=16 * 2**20, transcendentals=0),
        name="fetch",
    )(plan, vals)


def sum_tiles(part, plan_ref, vals_ref, table_ref, own_ref, away_refs, acc, prods):
    tile = vals_ref.shape[-1]

    def group(g, _):
        entries = [g * GROUP + i for i in range(GROUP)]
        for i, s in enumerate(entries):
            place = pl.multiple_of(plan_ref[4 * part + 2, s], tile)
            prods[i] = jnp.dot(
                vals_ref[plan_ref[4 * part, s]], table_ref[pl.ds(place, tile), :], preferred_element_type=jnp.float32
            )
        for i, s in enumerate(entries):
            row = pl.multiple_of(plan_ref[4 * part + 1, s], tile)
            acc[pl.ds(row, tile), :] += prods[i]
        return 0

    lax.fori_loop(0, (plan_ref[4 * part + 3, 0] + GROUP - 1) // GROUP, group, 0)
    size = own_ref.shape[0]
    own_ref[...] = acc[pl.ds(0, size), :]
    for k, ref in enumerate(away_refs):
        ref[...] = acc[pl.ds((k + 1) * size, size), :].astype(ref.dtype)


def far_kernel(n_pieces, plan_ref, vals_ref, *refs):
    pieces, refs = refs[:n_pieces], refs[n_pieces:]
    table_ref, own_ref, *away_refs = refs[:5]
    acc, prods, sem_table = refs[5:]
    copies, start = [], 0
    for i, piece in enumerate(pieces):
        rows = piece.shape[0]
        copies.append(pltpu.make_async_copy(piece, table_ref.at[pl.ds(start, rows)], sem_table.at[i]))
        copies[-1].start()
        start += rows
    acc[...] = jnp.zeros_like(acc)
    for copy in copies:
        copy.wait()
    sum_tiles(0, plan_ref, vals_ref, table_ref, own_ref, away_refs, acc, prods)


def near_kernel(plan_ref, vals_ref, table_ref, own_ref, *refs):
    acc, prods = refs[3:]
    acc[...] = jnp.zeros_like(acc)
    sum_tiles(1, plan_ref, vals_ref, table_ref, own_ref, refs[:3], acc, prods)


def aggregate(kernel, plan, vals, pieces, out_rows, with_table):
    slots, tile, _ = vals.shape
    feat = pieces[0].shape[1]
    table_rows = sum(piece.shape[0] for piece in pieces)
    n_x = lax.axis_size("x")
    vmem = pl.BlockSpec(memory_space=pltpu.VMEM)
    shape = (out_rows // n_x, feat)
    out = [jax.ShapeDtypeStruct(shape, jnp.float32)] + [jax.ShapeDtypeStruct(shape, jnp.bfloat16)] * (n_x - 1)
    scratch = [
        pltpu.VMEM((out_rows + tile, feat), jnp.float32),
        pltpu.VMEM((GROUP, tile, feat), jnp.float32),
    ]
    if with_table:
        out = [jax.ShapeDtypeStruct((table_rows, feat), jnp.bfloat16)] + out
        scratch.append(pltpu.SemaphoreType.DMA((len(pieces),)))
    near = pl.BlockSpec(memory_space=pl.ANY) if with_table else vmem
    return pl.pallas_call(
        kernel,
        out_shape=out,
        in_specs=[pl.BlockSpec(memory_space=pltpu.SMEM), vmem] + [near] * len(pieces),
        out_specs=[vmem] * len(out),
        scratch_shapes=scratch,
        compiler_params=pltpu.CompilerParams(vmem_limit_bytes=20 * 2**20),
        cost_estimate=pl.CostEstimate(flops=slots * tile * tile * feat, bytes_accessed=8 * 2**20, transcendentals=0),
        name="far_rows" if with_table else "near_rows",
    )(plan, vals, *pieces)


def head_kernel(scale, core_ref, own_ref, far_ref, *refs):
    *more_refs, weight_ref, labels_ref, logits_ref, keep_ref, give_ref = refs
    total = own_ref[...]
    for ref in more_refs:
        total += ref[...].astype(jnp.float32)
    total += far_ref[...].astype(jnp.float32)
    upper = total.astype(jnp.bfloat16)
    lower = (total - upper.astype(jnp.float32)).astype(jnp.bfloat16)
    weight = weight_ref[...]
    by_feature = (((1,), (1,)), ((), ()))
    logits = lax.dot_general(weight, upper, by_feature, preferred_element_type=jnp.float32)
    logits += lax.dot_general(weight, lower, by_feature, preferred_element_type=jnp.float32)
    logits_ref[...] = logits
    labels = labels_ref[...]
    classes = lax.broadcasted_iota(jnp.int32, logits.shape, 0)
    residual = logits - (labels == classes).astype(jnp.float32)
    residual = jnp.where(labels >= 0, residual, 0.0).astype(jnp.bfloat16)
    grad = jnp.dot(residual, upper, preferred_element_type=jnp.float32)
    grad += jnp.dot(residual, lower, preferred_element_type=jnp.float32)
    grad = grad * scale
    half = keep_ref.shape[0]
    first, second = grad[:half], grad[half:]
    second = jnp.concatenate([second, jnp.zeros((2 * half - grad.shape[0], grad.shape[1]), grad.dtype)], 0)
    swap = core_ref[0] == 1
    keep_ref[...] = jnp.where(swap, second, first)
    give_ref[...] = jnp.where(swap, first, second)


def head(core, own, far, more, weight, labels, scale):
    rows, feat = far.shape
    classes = weight.shape[0]
    half = (classes + 15) // 16 * 8
    vmem = pl.BlockSpec(memory_space=pltpu.VMEM)
    return pl.pallas_call(
        lambda *refs: head_kernel(scale, *refs),
        out_shape=(
            jax.ShapeDtypeStruct((classes, rows), jnp.float32),
            jax.ShapeDtypeStruct((half, feat), jnp.float32),
            jax.ShapeDtypeStruct((half, feat), jnp.float32),
        ),
        in_specs=[pl.BlockSpec(memory_space=pltpu.SMEM)] + [vmem] * (4 + len(more)),
        out_specs=(vmem, vmem, vmem),
        compiler_params=pltpu.CompilerParams(vmem_limit_bytes=32 * 2**20),
        name="head",
    )(core, own, far, *more, weight, labels)


def after(value, token):
    return jnp.where(token[0] < 0, jnp.zeros_like(value), value)


def gather_features(features, planned, fetched):
    by_z = jnp.concatenate([features] + [shift(features, "zl", -k) for k in (1, 2, 3)], 0)
    opposite = after(shift(features, "y", 2), planned)
    opposite = jnp.concatenate([opposite] + [shift(opposite, "zl", -k) for k in (1, 2, 3)], 0)
    mine = [by_z, shift(by_z, "y", -1), opposite, shift(by_z, "y", 1)]
    return mine + [shift(piece, "core", 1) for piece in [after(by_z, fetched)] + mine[1:]]


def sum_everywhere(keep, give, core, classes):
    total = keep + shift(give, "core", 1)
    for axis in ("y", "x"):
        total = (total + shift(total, axis, 2)) + (shift(total, axis, 1) + shift(total, axis, 3))
    total = total + shift(total, "zh", 1)
    total = (total + shift_z(total, 2)) + (shift_z(total, 1) + shift_z(total, -1))
    rest = shift(total, "core", 1)
    swap = core == 1
    return jnp.concatenate([jnp.where(swap, rest, total), jnp.where(swap, total, rest)], 0)[:classes]


def local(features, weight, labels, tile_rows, tile_cols, tile_count, tile_vals):
    tile = tile_vals.shape[-1]
    slots = tile_vals.shape[2]
    classes = weight.shape[1]
    nodes = features.shape[0]
    vals = pltpu.with_memory_space_constraint(tile_vals.reshape(slots, tile, tile), pltpu.HBM)
    out_rows = nodes * lax.axis_size("x")
    core = lax.axis_index("core").astype(jnp.int32)
    lists = plan(
        tile_rows.reshape(1, slots), tile_cols.reshape(1, slots), tile_count.reshape(1), nodes // tile, tile
    )

    vals, fetched = fetch(lists, vals)
    pieces = gather_features(features, lists[3], fetched)
    table, own, *away = aggregate(functools.partial(far_kernel, len(pieces)), lists, vals, pieces, out_rows, True)
    give = own + sum(shift(away[k], "x", k + 1).astype(jnp.float32) for k in (1, 0, 2))
    own, *away = aggregate(near_kernel, lists, vals, [table], out_rows, False)
    more = [shift(away[k], "x", k + 1) for k in (1, 0, 2)]
    far = shift(give.astype(jnp.bfloat16), "zh", 1)
    scale = 1.0 / math.sqrt(nodes * lax.axis_size(AXES))
    logits, keep, give = head(core.reshape(1), own, far, more, weight.T, labels.reshape(1, nodes), scale)
    return logits.T, sum_everywhere(keep, give, core, classes).T


def solution(mesh):
    fine = Mesh(mesh.devices.reshape(SIZES), AXES)
    placed = (
        P(COL + ROW, None),
        P(),
        P(AXES),
        P(ROW, COL, None),
        P(ROW, COL, None),
        P(ROW, COL),
        P(ROW, COL, None, None, None),
    )
    return jax.shard_map(
        local, mesh=fine, in_specs=placed, out_specs=(P(AXES, None), P()), check_vma=False
    )
```

```python
import functools
import math

import jax
import jax.numpy as jnp
from jax import lax
from jax.experimental import pallas as pl
from jax.experimental.pallas import tpu as pltpu
from jax.sharding import Mesh, PartitionSpec as P

AXES = ("y", "zl", "core", "x", "zh")
SIZES = (4, 4, 2, 4, 2)
ROW = AXES[:3]
COL = AXES[3:]
GROUP = 32
CHUNK = 32


def shift(value, axes, step):
    n = lax.axis_size(axes)
    return lax.ppermute(value, axes, [(i, (i + step) % n) for i in range(n)])


def shift_z(value, step):
    n_lo, n_hi = lax.axis_size("zl"), lax.axis_size("zh")
    n = n_lo * n_hi
    at = lambda z: (z % n_lo) * n_hi + z // n_lo
    return lax.ppermute(value, ("zl", "zh"), [(at(z), at((z + step) % n)) for z in range(n)])


def plan_kernel(per_device, tile, count_ref, rows_ref, cols_ref, plan_ref, token_ref):
    y0, z0, core0, x0, zh0 = (lax.axis_index(axis) for axis in AXES)
    count = count_ref[0]
    slots = rows_ref.shape[1]
    token_ref[0] = count
    slot = lax.broadcasted_iota(jnp.int32, (1, slots), 1)
    device, part = rows_ref[...] // per_device, rows_ref[...] % per_device
    row = (device // 2 - x0) % 4 * per_device + part
    far = (device % 2 - zh0) % 2 == 1
    device, part = cols_ref[...] // per_device, cols_ref[...] % per_device
    place = (device % 2 - core0) % 2 * 4 + (device // 8 - y0) % 4
    place = (place * 4 + (device // 2 % 4 - z0) % 4) * per_device + part
    used = slot < count
    before = lax.broadcasted_iota(jnp.int32, (slots, slots), 0) <= lax.broadcasted_iota(jnp.int32, (slots, slots), 1)
    before = before.astype(jnp.bfloat16)
    listed = lax.broadcasted_iota(jnp.int32, (slots, slots), 0)
    blank = jnp.zeros((5, slots), jnp.float32)
    values = jnp.concatenate([v.astype(jnp.float32) for v in (slot, row, place)] + [blank], 0).astype(jnp.bfloat16)
    by_slot = (((1,), (1,)), ((), ()))
    for k, member in enumerate((used & far, used & jnp.logical_not(far))):
        marks = jnp.broadcast_to(member.astype(jnp.float32), (8, slots)).astype(jnp.bfloat16)
        rank = jnp.dot(marks, before, preferred_element_type=jnp.float32)[:1].astype(jnp.int32)
        size = jnp.max(rank, axis=1, keepdims=True)
        rank = jnp.where(member, rank - 1, -1)
        picks = (listed == rank).astype(jnp.float32).astype(jnp.bfloat16)
        chosen = lax.dot_general(values, picks, by_slot, preferred_element_type=jnp.float32).astype(jnp.int32)
        filled = slot < size
        plan_ref[pl.ds(4 * k, 1), :] = chosen[0:1]
        plan_ref[pl.ds(4 * k + 1, 1), :] = jnp.where(filled, chosen[1:2], 4 * per_device) * tile
        plan_ref[pl.ds(4 * k + 2, 1), :] = chosen[2:3] * tile
        plan_ref[pl.ds(4 * k + 3, 1), :] = jnp.broadcast_to(size, (1, slots))


def plan(tile_rows, tile_cols, count, per_device, tile):
    slots = tile_rows.shape[1]
    vmem = pl.BlockSpec(memory_space=pltpu.VMEM)
    return pl.pallas_call(
        lambda *refs: plan_kernel(per_device, tile, *refs),
        out_shape=(jax.ShapeDtypeStruct((8, slots), jnp.int32), jax.ShapeDtypeStruct((1,), jnp.int32)),
        in_specs=[pl.BlockSpec(memory_space=pltpu.SMEM), vmem, vmem],
        out_specs=(vmem, pl.BlockSpec(memory_space=pltpu.SMEM)),
        name="plan",
    )(count, tile_rows, tile_cols)


def fetch_kernel(plan_ref, vals_ref, _, out_ref, token_ref, sems):
    count = plan_ref[3, 0] + plan_ref[7, 0]

    def each(act):
        for k in range(vals_ref.shape[0] // CHUNK):
            @pl.when(k * CHUNK < count)
            def _(k=k):
                part = pl.ds(k * CHUNK, CHUNK)
                act(pltpu.make_async_copy(vals_ref.at[part], out_ref.at[part], sems.at[k]))

    each(lambda copy: copy.start())
    each(lambda copy: copy.wait())
    token_ref[0] = count


def fetch(plan, vals, ready):
    smem = pl.BlockSpec(memory_space=pltpu.SMEM)
    return pl.pallas_call(
        fetch_kernel,
        out_shape=(jax.ShapeDtypeStruct(vals.shape, vals.dtype), jax.ShapeDtypeStruct((1,), jnp.int32)),
        in_specs=[smem, pl.BlockSpec(memory_space=pltpu.HBM), pl.BlockSpec(memory_space=pl.ANY)],
        out_specs=(pl.BlockSpec(memory_space=pltpu.VMEM), smem),
        scratch_shapes=[pltpu.SemaphoreType.DMA((vals.shape[0] // CHUNK,))],
        compiler_params=pltpu.CompilerParams(vmem_limit_bytes=12 * 2**20),
        cost_estimate=pl.CostEstimate(flops=0, bytes_accessed=16 * 2**20, transcendentals=0),
        name="fetch",
    )(plan, vals, ready)


def sum_tiles(part, plan_ref, vals_ref, table_ref, own_ref, away_refs, acc, prods):
    tile = vals_ref.shape[-1]

    def group(g, _):
        entries = [g * GROUP + i for i in range(GROUP)]
        for i, s in enumerate(entries):
            place = pl.multiple_of(plan_ref[4 * part + 2, s], tile)
            prods[i] = jnp.dot(
                vals_ref[plan_ref[4 * part, s]], table_ref[pl.ds(place, tile), :], preferred_element_type=jnp.float32
            )
        for i, s in enumerate(entries):
            row = pl.multiple_of(plan_ref[4 * part + 1, s], tile)
            acc[pl.ds(row, tile), :] += prods[i]
        return 0

    lax.fori_loop(0, (plan_ref[4 * part + 3, 0] + GROUP - 1) // GROUP, group, 0)
    size = own_ref.shape[0]
    own_ref[...] = acc[pl.ds(0, size), :]
    for k, ref in enumerate(away_refs):
        ref[...] = acc[pl.ds((k + 1) * size, size), :].astype(ref.dtype)


def far_kernel(n_pieces, plan_ref, vals_ref, *refs):
    pieces, refs = refs[:n_pieces], refs[n_pieces:]
    table_ref, own_ref, *away_refs = refs[:5]
    acc, prods, sem_table = refs[5:]
    copies, start = [], 0
    for i, piece in enumerate(pieces):
        rows = piece.shape[0]
        copies.append(pltpu.make_async_copy(piece, table_ref.at[pl.ds(start, rows)], sem_table.at[i]))
        copies[-1].start()
        start += rows
    acc[...] = jnp.zeros_like(acc)
    for copy in copies:
        copy.wait()
    sum_tiles(0, plan_ref, vals_ref, table_ref, own_ref, away_refs, acc, prods)


def near_kernel(plan_ref, vals_ref, table_ref, own_ref, *refs):
    acc, prods = refs[3:]
    acc[...] = jnp.zeros_like(acc)
    sum_tiles(1, plan_ref, vals_ref, table_ref, own_ref, refs[:3], acc, prods)


def aggregate(kernel, plan, vals, pieces, out_rows, with_table):
    slots, tile, _ = vals.shape
    feat = pieces[0].shape[1]
    table_rows = sum(piece.shape[0] for piece in pieces)
    n_x = lax.axis_size("x")
    vmem = pl.BlockSpec(memory_space=pltpu.VMEM)
    shape = (out_rows // n_x, feat)
    out = [jax.ShapeDtypeStruct(shape, jnp.float32)] + [jax.ShapeDtypeStruct(shape, jnp.bfloat16)] * (n_x - 1)
    scratch = [
        pltpu.VMEM((out_rows + tile, feat), jnp.float32),
        pltpu.VMEM((GROUP, tile, feat), jnp.float32),
    ]
    if with_table:
        out = [jax.ShapeDtypeStruct((table_rows, feat), jnp.bfloat16)] + out
        scratch.append(pltpu.SemaphoreType.DMA((len(pieces),)))
    near = pl.BlockSpec(memory_space=pl.ANY) if with_table else vmem
    return pl.pallas_call(
        kernel,
        out_shape=out,
        in_specs=[pl.BlockSpec(memory_space=pltpu.SMEM), vmem] + [near] * len(pieces),
        out_specs=[vmem] * len(out),
        scratch_shapes=scratch,
        compiler_params=pltpu.CompilerParams(vmem_limit_bytes=20 * 2**20),
        cost_estimate=pl.CostEstimate(flops=slots * tile * tile * feat, bytes_accessed=8 * 2**20, transcendentals=0),
        name="far_rows" if with_table else "near_rows",
    )(plan, vals, *pieces)


def head_kernel(scale, core_ref, own_ref, far_ref, *refs):
    *more_refs, weight_ref, labels_ref, logits_ref, keep_ref, give_ref = refs
    total = own_ref[...]
    for ref in more_refs:
        total += ref[...].astype(jnp.float32)
    total += far_ref[...].astype(jnp.float32)
    upper = total.astype(jnp.bfloat16)
    lower = (total - upper.astype(jnp.float32)).astype(jnp.bfloat16)
    weight = weight_ref[...]
    by_feature = (((1,), (1,)), ((), ()))
    logits = lax.dot_general(weight, upper, by_feature, preferred_element_type=jnp.float32)
    logits += lax.dot_general(weight, lower, by_feature, preferred_element_type=jnp.float32)
    logits_ref[...] = logits
    labels = labels_ref[...]
    classes = lax.broadcasted_iota(jnp.int32, logits.shape, 0)
    residual = logits - (labels == classes).astype(jnp.float32)
    residual = jnp.where(labels >= 0, residual, 0.0).astype(jnp.bfloat16)
    grad = jnp.dot(residual, upper, preferred_element_type=jnp.float32)
    grad += jnp.dot(residual, lower, preferred_element_type=jnp.float32)
    grad = grad * scale
    half = keep_ref.shape[0]
    first, second = grad[:half], grad[half:]
    second = jnp.concatenate([second, jnp.zeros((2 * half - grad.shape[0], grad.shape[1]), grad.dtype)], 0)
    swap = core_ref[0] == 1
    keep_ref[...] = jnp.where(swap, second, first)
    give_ref[...] = jnp.where(swap, first, second)


def head(core, own, far, more, weight, labels, scale):
    rows, feat = far.shape
    classes = weight.shape[0]
    half = (classes + 15) // 16 * 8
    vmem = pl.BlockSpec(memory_space=pltpu.VMEM)
    return pl.pallas_call(
        lambda *refs: head_kernel(scale, *refs),
        out_shape=(
            jax.ShapeDtypeStruct((classes, rows), jnp.float32),
            jax.ShapeDtypeStruct((half, feat), jnp.float32),
            jax.ShapeDtypeStruct((half, feat), jnp.float32),
        ),
        in_specs=[pl.BlockSpec(memory_space=pltpu.SMEM)] + [vmem] * (4 + len(more)),
        out_specs=(vmem, vmem, vmem),
        compiler_params=pltpu.CompilerParams(vmem_limit_bytes=32 * 2**20),
        name="head",
    )(core, own, far, *more, weight, labels)


def after(value, token):
    return jnp.where(token[0] < 0, jnp.zeros_like(value), value)


def gather_features(features, lists, planned, vals):
    by_z = jnp.concatenate([features] + [shift(features, "zl", -k) for k in (1, 2, 3)], 0)
    opposite = after(shift(features, "y", 2), planned)
    late = jnp.where(by_z[-1, 0] + by_z[features.shape[0], 0] > 1e30, jnp.zeros_like(opposite), opposite)
    opposite = jnp.concatenate([opposite] + [shift(late, "zl", -k) for k in (1, 2, 3)], 0)
    mine = [by_z, shift(by_z, "y", -1), opposite, shift(by_z, "y", 1)]
    vals, fetched = fetch(lists, vals, by_z)
    return vals, mine + [shift(piece, "core", 1) for piece in [after(by_z, fetched)] + mine[1:]]


def sum_everywhere(keep, give, core, classes):
    total = keep + shift(give, "core", 1)
    for axis in ("y", "x"):
        total = (total + shift(total, axis, 2)) + (shift(total, axis, 1) + shift(total, axis, 3))
    total = total + shift(total, "zh", 1)
    total = (total + shift_z(total, 2)) + (shift_z(total, 1) + shift_z(total, -1))
    rest = shift(total, "core", 1)
    swap = core == 1
    return jnp.concatenate([jnp.where(swap, rest, total), jnp.where(swap, total, rest)], 0)[:classes]


def local(features, weight, labels, tile_rows, tile_cols, tile_count, tile_vals):
    tile = tile_vals.shape[-1]
    slots = tile_vals.shape[2]
    classes = weight.shape[1]
    nodes = features.shape[0]
    vals = pltpu.with_memory_space_constraint(tile_vals.reshape(slots, tile, tile), pltpu.HBM)
    out_rows = nodes * lax.axis_size("x")
    core = lax.axis_index("core").astype(jnp.int32)
    lists, planned = plan(
        tile_rows.reshape(1, slots), tile_cols.reshape(1, slots), tile_count.reshape(1), nodes // tile, tile
    )

    vals, pieces = gather_features(features, lists, planned, vals)
    table, own, *away = aggregate(functools.partial(far_kernel, len(pieces)), lists, vals, pieces, out_rows, True)
    give = own + sum(shift(away[k], "x", k + 1).astype(jnp.float32) for k in (1, 0, 2))
    own, *away = aggregate(near_kernel, lists, vals, [table], out_rows, False)
    more = [shift(away[k], "x", k + 1) for k in (1, 0, 2)]
    far = shift(give.astype(jnp.bfloat16), "zh", 1)
    scale = 1.0 / math.sqrt(nodes * lax.axis_size(AXES))
    logits, keep, give = head(core.reshape(1), own, far, more, weight.T, labels.reshape(1, nodes), scale)
    return logits.T, sum_everywhere(keep, give, core, classes).T


def solution(mesh):
    fine = Mesh(mesh.devices.reshape(SIZES), AXES)
    placed = (
        P(COL + ROW, None),
        P(),
        P(AXES),
        P(ROW, COL, None),
        P(ROW, COL, None),
        P(ROW, COL),
        P(ROW, COL, None, None, None),
    )
    return jax.shard_map(
        local, mesh=fine, in_specs=placed, out_specs=(P(AXES, None), P()), check_vma=False
    )
```

```python
import functools
import math

import jax
import jax.numpy as jnp
from jax import lax
from jax.experimental import pallas as pl
from jax.experimental.pallas import tpu as pltpu
from jax.sharding import Mesh, PartitionSpec as P

AXES = ("y", "zl", "core", "x", "zh")
SIZES = (4, 4, 2, 4, 2)
ROW = AXES[:3]
COL = AXES[3:]
GROUP = 32
CHUNK = 32


def shift(value, axes, step):
    n = lax.axis_size(axes)
    return lax.ppermute(value, axes, [(i, (i + step) % n) for i in range(n)])


def shift_z(value, step):
    n_lo, n_hi = lax.axis_size("zl"), lax.axis_size("zh")
    n = n_lo * n_hi
    at = lambda z: (z % n_lo) * n_hi + z // n_lo
    return lax.ppermute(value, ("zl", "zh"), [(at(z), at((z + step) % n)) for z in range(n)])


def plan_kernel(per_device, tile, count_ref, rows_ref, cols_ref, plan_ref, token_ref):
    y0, z0, core0, x0, zh0 = (lax.axis_index(axis) for axis in AXES)
    count = count_ref[0]
    slots = rows_ref.shape[1]
    token_ref[0] = count
    slot = lax.broadcasted_iota(jnp.int32, (1, slots), 1)
    device, part = rows_ref[...] // per_device, rows_ref[...] % per_device
    row = (device // 2 - x0) % 4 * per_device + part
    far = (device % 2 - zh0) % 2 == 1
    device, part = cols_ref[...] // per_device, cols_ref[...] % per_device
    y, z = (device // 8 - y0) % 4, (device // 2 % 4 - z0) % 4
    z = jnp.where((y == 2) & (z >= 2), 5 - z, z)
    place = (((device % 2 - core0) % 2 * 4 + y) * 4 + z) * per_device + part
    used = slot < count
    before = lax.broadcasted_iota(jnp.int32, (slots, slots), 0) <= lax.broadcasted_iota(jnp.int32, (slots, slots), 1)
    before = before.astype(jnp.bfloat16)
    listed = lax.broadcasted_iota(jnp.int32, (slots, slots), 0)
    blank = jnp.zeros((5, slots), jnp.float32)
    values = jnp.concatenate([v.astype(jnp.float32) for v in (slot, row, place)] + [blank], 0).astype(jnp.bfloat16)
    by_slot = (((1,), (1,)), ((), ()))
    for k, member in enumerate((used & far, used & jnp.logical_not(far))):
        marks = jnp.broadcast_to(member.astype(jnp.float32), (8, slots)).astype(jnp.bfloat16)
        rank = jnp.dot(marks, before, preferred_element_type=jnp.float32)[:1].astype(jnp.int32)
        size = jnp.max(rank, axis=1, keepdims=True)
        rank = jnp.where(member, rank - 1, -1)
        picks = (listed == rank).astype(jnp.float32).astype(jnp.bfloat16)
        chosen = lax.dot_general(values, picks, by_slot, preferred_element_type=jnp.float32).astype(jnp.int32)
        filled = slot < size
        plan_ref[pl.ds(4 * k, 1), :] = chosen[0:1]
        plan_ref[pl.ds(4 * k + 1, 1), :] = jnp.where(filled, chosen[1:2], 4 * per_device) * tile
        plan_ref[pl.ds(4 * k + 2, 1), :] = chosen[2:3] * tile
        plan_ref[pl.ds(4 * k + 3, 1), :] = jnp.broadcast_to(size, (1, slots))


def plan(tile_rows, tile_cols, count, per_device, tile):
    slots = tile_rows.shape[1]
    vmem = pl.BlockSpec(memory_space=pltpu.VMEM)
    return pl.pallas_call(
        lambda *refs: plan_kernel(per_device, tile, *refs),
        out_shape=(jax.ShapeDtypeStruct((8, slots), jnp.int32), jax.ShapeDtypeStruct((1,), jnp.int32)),
        in_specs=[pl.BlockSpec(memory_space=pltpu.SMEM), vmem, vmem],
        out_specs=(vmem, pl.BlockSpec(memory_space=pltpu.SMEM)),
        name="plan",
    )(count, tile_rows, tile_cols)


def fetch_kernel(plan_ref, vals_ref, _, out_ref, token_ref, sems):
    count = plan_ref[3, 0] + plan_ref[7, 0]

    def each(act):
        for k in range(vals_ref.shape[0] // CHUNK):
            @pl.when(k * CHUNK < count)
            def _(k=k):
                part = pl.ds(k * CHUNK, CHUNK)
                act(pltpu.make_async_copy(vals_ref.at[part], out_ref.at[part], sems.at[k]))

    each(lambda copy: copy.start())
    each(lambda copy: copy.wait())
    token_ref[0] = count


def fetch(plan, vals, ready):
    smem = pl.BlockSpec(memory_space=pltpu.SMEM)
    return pl.pallas_call(
        fetch_kernel,
        out_shape=(jax.ShapeDtypeStruct(vals.shape, vals.dtype), jax.ShapeDtypeStruct((1,), jnp.int32)),
        in_specs=[smem, pl.BlockSpec(memory_space=pltpu.HBM), pl.BlockSpec(memory_space=pl.ANY)],
        out_specs=(pl.BlockSpec(memory_space=pltpu.VMEM), smem),
        scratch_shapes=[pltpu.SemaphoreType.DMA((vals.shape[0] // CHUNK,))],
        compiler_params=pltpu.CompilerParams(vmem_limit_bytes=12 * 2**20),
        cost_estimate=pl.CostEstimate(flops=0, bytes_accessed=16 * 2**20, transcendentals=0),
        name="fetch",
    )(plan, vals, ready)


def sum_tiles(part, plan_ref, vals_ref, table_ref, own_ref, away_refs, acc, prods):
    tile = vals_ref.shape[-1]

    def group(g, _):
        entries = [g * GROUP + i for i in range(GROUP)]
        for i, s in enumerate(entries):
            place = pl.multiple_of(plan_ref[4 * part + 2, s], tile)
            prods[i] = jnp.dot(
                vals_ref[plan_ref[4 * part, s]], table_ref[pl.ds(place, tile), :], preferred_element_type=jnp.float32
            )
        for i, s in enumerate(entries):
            row = pl.multiple_of(plan_ref[4 * part + 1, s], tile)
            acc[pl.ds(row, tile), :] += prods[i]
        return 0

    lax.fori_loop(0, (plan_ref[4 * part + 3, 0] + GROUP - 1) // GROUP, group, 0)
    size = own_ref.shape[0]
    own_ref[...] = acc[pl.ds(0, size), :]
    for k, ref in enumerate(away_refs):
        ref[...] = acc[pl.ds((k + 1) * size, size), :].astype(ref.dtype)


def far_kernel(n_pieces, plan_ref, vals_ref, *refs):
    pieces, refs = refs[:n_pieces], refs[n_pieces:]
    table_ref, own_ref, *away_refs = refs[:5]
    acc, prods, sem_table = refs[5:]
    copies, start = [], 0
    for i, piece in enumerate(pieces):
        rows = piece.shape[0]
        copies.append(pltpu.make_async_copy(piece, table_ref.at[pl.ds(start, rows)], sem_table.at[i]))
        copies[-1].start()
        start += rows
    acc[...] = jnp.zeros_like(acc)
    for copy in copies:
        copy.wait()
    sum_tiles(0, plan_ref, vals_ref, table_ref, own_ref, away_refs, acc, prods)


def near_kernel(plan_ref, vals_ref, table_ref, own_ref, *refs):
    acc, prods = refs[3:]
    acc[...] = jnp.zeros_like(acc)
    sum_tiles(1, plan_ref, vals_ref, table_ref, own_ref, refs[:3], acc, prods)


def aggregate(kernel, plan, vals, pieces, out_rows, with_table):
    slots, tile, _ = vals.shape
    feat = pieces[0].shape[1]
    table_rows = sum(piece.shape[0] for piece in pieces)
    n_x = lax.axis_size("x")
    vmem = pl.BlockSpec(memory_space=pltpu.VMEM)
    shape = (out_rows // n_x, feat)
    out = [jax.ShapeDtypeStruct(shape, jnp.float32)] + [jax.ShapeDtypeStruct(shape, jnp.bfloat16)] * (n_x - 1)
    scratch = [
        pltpu.VMEM((out_rows + tile, feat), jnp.float32),
        pltpu.VMEM((GROUP, tile, feat), jnp.float32),
    ]
    if with_table:
        out = [jax.ShapeDtypeStruct((table_rows, feat), jnp.bfloat16)] + out
        scratch.append(pltpu.SemaphoreType.DMA((len(pieces),)))
    near = pl.BlockSpec(memory_space=pl.ANY) if with_table else vmem
    return pl.pallas_call(
        kernel,
        out_shape=out,
        in_specs=[pl.BlockSpec(memory_space=pltpu.SMEM), vmem] + [near] * len(pieces),
        out_specs=[vmem] * len(out),
        scratch_shapes=scratch,
        compiler_params=pltpu.CompilerParams(vmem_limit_bytes=20 * 2**20),
        cost_estimate=pl.CostEstimate(flops=slots * tile * tile * feat, bytes_accessed=8 * 2**20, transcendentals=0),
        name="far_rows" if with_table else "near_rows",
    )(plan, vals, *pieces)


def head_kernel(scale, core_ref, own_ref, far_ref, *refs):
    *more_refs, weight_ref, labels_ref, logits_ref, keep_ref, give_ref = refs
    total = own_ref[...]
    for ref in more_refs:
        total += ref[...].astype(jnp.float32)
    total += far_ref[...].astype(jnp.float32)
    upper = total.astype(jnp.bfloat16)
    lower = (total - upper.astype(jnp.float32)).astype(jnp.bfloat16)
    weight = weight_ref[...]
    by_feature = (((1,), (1,)), ((), ()))
    logits = lax.dot_general(weight, upper, by_feature, preferred_element_type=jnp.float32)
    logits += lax.dot_general(weight, lower, by_feature, preferred_element_type=jnp.float32)
    logits_ref[...] = logits
    labels = labels_ref[...]
    classes = lax.broadcasted_iota(jnp.int32, logits.shape, 0)
    residual = logits - (labels == classes).astype(jnp.float32)
    residual = jnp.where(labels >= 0, residual, 0.0).astype(jnp.bfloat16)
    grad = jnp.dot(residual, upper, preferred_element_type=jnp.float32)
    grad += jnp.dot(residual, lower, preferred_element_type=jnp.float32)
    grad = grad * scale
    half = keep_ref.shape[0]
    first, second = grad[:half], grad[half:]
    second = jnp.concatenate([second, jnp.zeros((2 * half - grad.shape[0], grad.shape[1]), grad.dtype)], 0)
    swap = core_ref[0] == 1
    keep_ref[...] = jnp.where(swap, second, first)
    give_ref[...] = jnp.where(swap, first, second)


def head(core, own, far, more, weight, labels, scale):
    rows, feat = far.shape
    classes = weight.shape[0]
    half = (classes + 15) // 16 * 8
    vmem = pl.BlockSpec(memory_space=pltpu.VMEM)
    return pl.pallas_call(
        lambda *refs: head_kernel(scale, *refs),
        out_shape=(
            jax.ShapeDtypeStruct((classes, rows), jnp.float32),
            jax.ShapeDtypeStruct((half, feat), jnp.float32),
            jax.ShapeDtypeStruct((half, feat), jnp.float32),
        ),
        in_specs=[pl.BlockSpec(memory_space=pltpu.SMEM)] + [vmem] * (4 + len(more)),
        out_specs=(vmem, vmem, vmem),
        compiler_params=pltpu.CompilerParams(vmem_limit_bytes=32 * 2**20),
        name="head",
    )(core, own, far, *more, weight, labels)


def after(value, token):
    return jnp.where(token[0] < 0, jnp.zeros_like(value), value)


def gather_features(features, lists, planned, vals):
    by_z = jnp.concatenate([features] + [shift(features, "zl", -k) for k in (1, 2, 3)], 0)
    opposite = after(shift(features, "y", 2), planned)
    late = jnp.where(by_z[-1, 0] + by_z[features.shape[0], 0] > 1e30, jnp.zeros_like(opposite), opposite)
    opposite = jnp.concatenate([opposite] + [shift(late, "zl", -k) for k in (1, 3, 2)], 0)
    mine = [by_z, shift(by_z, "y", -1), opposite, shift(by_z, "y", 1)]
    vals, fetched = fetch(lists, vals, by_z)
    return vals, mine + [shift(piece, "core", 1) for piece in [after(by_z, fetched)] + mine[1:]]


def sum_everywhere(keep, give, core, classes):
    total = keep + shift(give, "core", 1)
    for axis in ("y", "x"):
        total = (total + shift(total, axis, 2)) + (shift(total, axis, 1) + shift(total, axis, 3))
    total = total + shift(total, "zh", 1)
    total = (total + shift_z(total, 2)) + (shift_z(total, 1) + shift_z(total, -1))
    rest = shift(total, "core", 1)
    swap = core == 1
    return jnp.concatenate([jnp.where(swap, rest, total), jnp.where(swap, total, rest)], 0)[:classes]


def local(features, weight, labels, tile_rows, tile_cols, tile_count, tile_vals):
    tile = tile_vals.shape[-1]
    slots = tile_vals.shape[2]
    classes = weight.shape[1]
    nodes = features.shape[0]
    vals = pltpu.with_memory_space_constraint(tile_vals.reshape(slots, tile, tile), pltpu.HBM)
    out_rows = nodes * lax.axis_size("x")
    core = lax.axis_index("core").astype(jnp.int32)
    lists, planned = plan(
        tile_rows.reshape(1, slots), tile_cols.reshape(1, slots), tile_count.reshape(1), nodes // tile, tile
    )

    vals, pieces = gather_features(features, lists, planned, vals)
    table, own, *away = aggregate(functools.partial(far_kernel, len(pieces)), lists, vals, pieces, out_rows, True)
    give = own + sum(shift(away[k], "x", k + 1).astype(jnp.float32) for k in (1, 0, 2))
    own, *away = aggregate(near_kernel, lists, vals, [table], out_rows, False)
    more = [shift(away[k], "x", k + 1) for k in (1, 0, 2)]
    far = shift(give.astype(jnp.bfloat16), "zh", 1)
    scale = 1.0 / math.sqrt(nodes * lax.axis_size(AXES))
    logits, keep, give = head(core.reshape(1), own, far, more, weight.T, labels.reshape(1, nodes), scale)
    return logits.T, sum_everywhere(keep, give, core, classes).T


def solution(mesh):
    fine = Mesh(mesh.devices.reshape(SIZES), AXES)
    placed = (
        P(COL + ROW, None),
        P(),
        P(AXES),
        P(ROW, COL, None),
        P(ROW, COL, None),
        P(ROW, COL),
        P(ROW, COL, None, None, None),
    )
    return jax.shard_map(
        local, mesh=fine, in_specs=placed, out_specs=(P(AXES, None), P()), check_vma=False
    )
```
